1024 devices in a mesh: pipe: 8 (over z), expert: 32 (over y, x_lo, core), dp: 4 (over x_hi).
Axes of the slice: x: 8 (x_hi: 4, x_lo: 2; x = x_hi * 2 + x_lo), y: 8, z: 8, core: 2. Of those that a mesh axis runs over, the one named last changes fastest.
Arguments:
- tokens: bfloat16 [8, 4096, 3584], P('pipe', 'expert', 'dp'), may hold values from -6 to 6
- expert_ids: int32 [8, 4096, 2], P('pipe', 'expert'), may hold values from 0 to 31, all different within a row; in each aligned block of 128 rows (0 to 127, 128 to 255, ..., all dimensions but the last counted through in order) at most 16 rows name the same one
- gate_levels: int32 [8, 4096, 2], P('pipe', 'expert'), may hold values from 1 to 255
- gain: bfloat16 [3584], P('dp'), may hold values from 0.5 to 2
- w_gate: bfloat16 [32, 3584, 1024], P('expert', None, 'dp'), may hold values from -0.09375 to 0.09375
- w_up: bfloat16 [32, 3584, 1024], P('expert', None, 'dp'), may hold values from -0.09375 to 0.09375
- w_down: bfloat16 [32, 1024, 3584], P('expert', 'dp'), may hold values from -0.1875 to 0.1875
Outputs:
- next_input: bfloat16 [8, 4096, 3584], P('pipe', 'expert', 'dp')
The draws below stay inside these ranges and needn't reach their ends.
Inputs may be any that keep to these rules, and one draw needn't show every extreme that they name: `expert_ids`: each token names 2 different experts. Within each aligned block of 128 tokens of a section, no expert is named by more than 16 tokens, and in every draw some expert is named by exactly 16 tokens of some block.
All inputs are finite; a program needn't handle non-finite values.
Results may differ from the reference program's by a relative error of at most 0.012.
Values may be sent and summed in bfloat16 or wider, within the bound.
A program may use at most 32 MiB of HBM per device.

```python
import math
import jax
import jax.numpy as jnp
import numpy as np
from jax import lax

D = 3584
FF = 1024
TOPW = 2
TOK_DEV = 128
EXPERTS = 32
TOKENS = 4096
CAP = 16
N_PIPE = 8
N_DP = 4


def touch_ends(values, stream_key, low, largest):
    dims = values.shape
    place = [jax.random.randint(jax.random.fold_in(stream_key, axis), (), 0, dims[axis]) for axis in range(len(dims))]
    values = values.at[tuple(place)].set(low)
    longest = dims.index(max(dims))
    place[longest] = (place[longest] + 1) % dims[longest]
    return values.at[tuple(place)].set(largest)


def block_scale(stream_key, shape, cuts, low, top_value):
    def one(position, blocks):
        heights = jax.random.uniform(jax.random.fold_in(jax.random.fold_in(stream_key, 6), position), (blocks,), jnp.float32, low / len(cuts), top_value / len(cuts))
        return jnp.repeat(jnp.exp(heights), shape[position] // blocks).reshape((-1,) + (1,) * (len(shape) - position - 1))

    factor_of = one(*cuts[0])
    for cut in cuts[1:]:
        factor_of = factor_of * one(*cut)
    return factor_of


def deal_out(stream_key, own, number, rows, number_of, top, bound, lean):
    sequence = jax.random.permutation(stream_key, number_of)
    crowded, usual = load_shares(number_of, rows * top, bound, lean, True), load_shares(number_of, rows * top, bound, lean, False)
    places = jnp.arange(number_of)

    def named(sizes, rotation):
        used = int((sizes > 0).sum())
        fixed = max(1, used // 4)
        moved = fixed + (places - fixed + rotation * (used - fixed)) % max(1, number_of - fixed)
        return jnp.zeros((number_of,), jnp.int32).at[sequence[jnp.where(places < fixed, places, moved)]].set(jnp.asarray(sizes, jnp.int32))

    sizes = jnp.where(number % 4 == 0, named(crowded, number // 4), named(usual, number - number // 4 - 1))
    mixed = jax.random.permutation(jax.random.fold_in(own, 3), number_of)
    source_of, receiver = mixed[0:number_of // 2 * 2:2], mixed[1:number_of // 2 * 2:2]
    room = jnp.minimum(sizes[source_of] - 1, bound - sizes[receiver]) // 2
    room = jnp.where((source_of == sequence[0]) | (receiver == sequence[0]) | (sizes[receiver] == 0), 0, jnp.maximum(room, 0))
    moved = jax.random.randint(jax.random.fold_in(own, 4), (number_of // 2,), 0, 1 << 20) % (room + 1)
    sizes = sizes.at[source_of].add(-moved).at[receiver].add(moved)
    members = jnp.searchsorted(jnp.cumsum(sizes), jnp.arange(rows * top), side="right").astype(jnp.int32)
    grid = members.reshape(top, rows).T
    grid = grid[jax.random.permutation(jax.random.fold_in(own, 1), rows)]
    rotation = jax.random.randint(jax.random.fold_in(own, 2), (rows, 1), 0, top)
    return jnp.take_along_axis(grid, (jnp.arange(top)[None, :] + rotation) % top, axis=1)


def load_shares(number_of, total, most, slope, full):
    loads = [(1 << 20) // math.isqrt(standing ** slope) + 1 for standing in range(1, number_of + 1)]
    largest = most if full else min(most, max(-(-total // number_of), total * loads[0] // sum(loads)))
    least = 1 if total - largest >= number_of - 1 else 0
    counts, rest = [largest] + [least] * (number_of - 1), total - largest - least * (number_of - 1)
    while rest > 0:
        movable = [i for i in range(1, number_of) if counts[i] < largest] or [i for i in range(1, number_of) if counts[i] < most]
        pool, remaining = sum([loads[i] for i in movable]), rest
        for i in movable:
            more = min(most - counts[i], max(1, remaining * loads[i] // pool), rest)
            counts[i] = counts[i] + more
            rest = rest - more
    return np.array(counts)


def noise(rng, extent, deviation, most, cuts=(), kind=jnp.bfloat16):
    entries = jax.random.normal(rng, extent, jnp.float32) * deviation
    if len(cuts) > 0:
        entries = block_scale(rng, extent, cuts, -0.22, 0.18) * entries
    return jnp.clip(entries, min=-most, max=most).astype(kind)


def setup_inputs(seed: int = 0) -> dict:
    arg_keys = jax.random.split(jax.random.key(seed), 8)
    tokens = noise(arg_keys[0], (N_PIPE, TOKENS, D), 1.0, 6.0, ((0, 8), (1, 32), (2, 4)))
    expert_ids_keys = jax.random.split(jax.random.fold_in(arg_keys[1], 1), N_PIPE * TOKENS // TOK_DEV)
    expert_ids_turns = jax.random.permutation(jax.random.fold_in(arg_keys[1], 3), N_PIPE * TOKENS // TOK_DEV)
    expert_ids = jax.vmap(lambda own, number: deal_out(jax.random.fold_in(arg_keys[1], 2), own, number, TOK_DEV, EXPERTS, TOPW, CAP, 2))(expert_ids_keys, expert_ids_turns).reshape((N_PIPE, TOKENS, TOPW))
    gate_levels = touch_ends(jax.random.randint(arg_keys[2], (N_PIPE, TOKENS, TOPW), 1, 256), jax.random.fold_in(arg_keys[2], 1), 1, 255).astype(jnp.int32)
    gain = jnp.clip(jnp.exp(math.log(2.0) - 1.3862944 * jax.random.uniform(arg_keys[3], (D,), jnp.float32) ** block_scale(arg_keys[3], (D,), ((0, 4),), -0.2, 0.2)), 0.5, 2.0).astype(jnp.bfloat16)
    w_gate = noise(arg_keys[4], (EXPERTS, D, FF), D ** -0.5, 0.09375, ((0, 32), (2, 4)))
    w_up = noise(arg_keys[5], (EXPERTS, D, FF), D ** -0.5, 0.09375, ((0, 32), (2, 4)))
    w_down = noise(arg_keys[6], (EXPERTS, FF, D), FF ** -0.5, 0.1875, ((0, 32), (1, 4)))
    return {"tokens": tokens, "expert_ids": expert_ids, "gate_levels": gate_levels, "gain": gain, "w_gate": w_gate, "w_up": w_up, "w_down": w_down}


epsilon = 1e-06

def expert_block(rows, gain, weights_gate, weights_up, weights_down):
    wide_rows = rows.astype(jnp.float32)
    squares = lax.optimization_barrier(jnp.sum(jnp.square(wide_rows), axis=1))
    inverse = lax.rsqrt(squares / D + epsilon)
    scaled = (wide_rows * gain.astype(jnp.float32)[None, :]).astype(jnp.bfloat16)
    gate_value = inverse[:, None] * jnp.dot(scaled, weights_gate, preferred_element_type=jnp.float32)
    up_value = inverse[:, None] * jnp.dot(scaled, weights_up, preferred_element_type=jnp.float32)
    hidden = (jax.nn.silu(gate_value) * up_value).astype(jnp.bfloat16)
    quarter = FF // N_DP
    combined = jnp.zeros((rows.shape[0], D), jnp.float32)
    for portion in range(N_DP):
        partial_sum = jnp.dot(hidden[:, portion * quarter:(portion + 1) * quarter], weights_down[portion * quarter:(portion + 1) * quarter, :], preferred_element_type=jnp.float32).astype(jnp.bfloat16)
        partial_sum = lax.optimization_barrier(partial_sum)
        combined = combined + partial_sum.astype(jnp.float32)
    return combined.astype(jnp.bfloat16)

def reference(tokens, expert_ids, gate_levels, gain, w_gate, w_up, w_down):
    blocks = TOKENS // TOK_DEV
    limit = blocks * CAP
    token_iota = jnp.arange(TOKENS, dtype=jnp.int32)
    expert_iota = jnp.arange(EXPERTS, dtype=jnp.int32)

    def section_layer(item):
        rows_all, choose, levels = item
        matches = (choose[:, :, None] == expert_iota[None, None, :]).astype(jnp.int32)
        member = lax.optimization_barrier(jnp.sum(matches, axis=1)).astype(jnp.int32)
        blocked = member.reshape(blocks, TOK_DEV, EXPERTS)
        before = (jnp.cumsum(blocked, axis=1).astype(jnp.int32) - blocked).reshape(TOKENS, EXPERTS)
        slot_full = ((token_iota // TOK_DEV)[:, None] * CAP + before).astype(jnp.int32)
        target = jnp.where(member == 1, slot_full, limit).astype(jnp.int32)
        table = jnp.full((EXPERTS, limit), TOKENS, jnp.int32)
        table = table.at[jnp.broadcast_to(expert_iota[None, :], (TOKENS, EXPERTS)), target].set(jnp.broadcast_to(token_iota[:, None], (TOKENS, EXPERTS)), mode='drop')
        padded = jnp.concatenate([rows_all, jnp.zeros((1, D), jnp.bfloat16)], axis=0)

        def per_expert(pieces):
            index_row, gate_mat, up_mat, down_mat = pieces
            return expert_block(padded[index_row], gain, gate_mat, up_mat, down_mat)
        outputs = lax.map(per_expert, (table, w_gate, w_up, w_down))
        slot_pick = jnp.take_along_axis(slot_full, choose, axis=1).astype(jnp.int32)
        picked = outputs[choose, slot_pick]
        wide_levels = levels.astype(jnp.float32)
        shares = wide_levels / lax.optimization_barrier(jnp.sum(wide_levels, axis=1, keepdims=True))
        result = rows_all.astype(jnp.float32) + lax.optimization_barrier(jnp.sum(shares[:, :, None] * picked.astype(jnp.float32), axis=1))
        return result.astype(jnp.bfloat16)
    layer_out = lax.map(section_layer, (tokens, expert_ids, gate_levels))
    return jnp.roll(layer_out, 1, axis=0)
```

```python
import functools

import jax
import jax.numpy as jnp
from jax import lax
from jax.experimental import pallas as pl
from jax.experimental.pallas import tpu as pltpu
from jax.sharding import PartitionSpec as P

MESH = pl.DeviceIdType.MESH
epsilon = 1e-06
bf16 = jnp.bfloat16
f32 = jnp.float32


def kernel(sizes, cap, ids_ref, lev_ref, tok_ref, gain_ref, wg_any, wu_any, wd_any, out_ref,
           wg, wu, wd, meta, meta_nb, meta_prev, meta_pnb, tok_nb, tok_prev, outb, gat, gains,
           part, rs_opp, rs_l, rs_r, res, ret, xp_out, xp_in,
           w_sem, disp_s, disp_r, ag_s, ag_r, rs_s, rs_rr, ret_s, ret_r, misc_s, misc_r):
    n_pipe, n_exp, n_dp = sizes
    group = n_exp // 2
    tokens, quarter = tok_ref.shape
    half_rows = group * cap
    chunk = half_rows // 2
    split = chunk // 2
    full_width = n_dp * quarter

    z = lax.axis_index("pipe")
    e = lax.axis_index("expert")
    d = lax.axis_index("dp")
    x_lo = lax.rem(lax.div(e, 2), 2)
    g = lax.div(e, 4) * 2 + lax.rem(e, 2)
    right, left = lax.rem(d + 1, n_dp), lax.rem(d + n_dp - 1, n_dp)
    z_next, z_prev = lax.rem(z + 1, n_pipe), lax.rem(z + n_pipe - 1, n_pipe)

    def member(i):
        return lax.div(i, 2) * 4 + x_lo * 2 + lax.rem(i, 2)

    def offset(s):
        return jnp.where(lax.rem(s, 2) == 1, lax.div(s + 1, 2), group - lax.div(s, 2))

    def ahead(s):
        return member(lax.rem(g + offset(s), group))

    def behind(s):
        return member(lax.rem(g + 2 * group - offset(s), group))

    across = lax.div(e, 4) * 4 + (1 - x_lo) * 2 + lax.rem(e, 2)

    barrier = pltpu.get_barrier_semaphore()

    def tell_group(s, carry):
        pl.semaphore_signal(barrier, inc=1, device_id=(z, ahead(s), d), device_id_type=MESH)
        return carry

    def tell_before(s, carry):
        pl.semaphore_signal(barrier, inc=1, device_id=(z_prev, ahead(s), d), device_id_type=MESH)
        return carry

    pl.semaphore_signal(barrier, inc=1, device_id=(z, across, d), device_id_type=MESH)
    pl.semaphore_signal(barrier, inc=1, device_id=(z, e, right), device_id_type=MESH)
    pl.semaphore_signal(barrier, inc=1, device_id=(z, e, left), device_id_type=MESH)
    lax.fori_loop(1, group, tell_group, 0)
    lax.fori_loop(0, group, tell_before, 0)

    quarters = [d, left, right, lax.rem(d + 2, n_dp)]
    loads = []
    for q in range(4):
        at = pl.ds(pl.multiple_of(quarters[q] * quarter, 128), quarter)
        loads.append(pltpu.make_async_copy(wg_any.at[at, :], wg.at[q], w_sem.at[3 * q]))
        loads.append(pltpu.make_async_copy(wu_any.at[at, :], wu.at[q], w_sem.at[3 * q + 1]))
        loads.append(pltpu.make_async_copy(wd_any.at[:, at], wd.at[q], w_sem.at[3 * q + 2]))
    for copy in loads:
        copy.start()

    def slots(meta_ref):
        i = lax.broadcasted_iota(jnp.int32, (group, tokens), 0)
        off = jnp.where((i & 1) == 1, (i + 1) >> 1, group - (i >> 1))
        return i, off

    def place(meta_ref, sign):
        i, off = slots(meta_ref)
        member_of = (g + 2 * group + sign * off) & (group - 1)
        expert = (member_of >> 1) * 4 + x_lo * 2 + (member_of & 1)
        first = meta_ref[0:1, :] == expert
        second = meta_ref[1:2, :] == expert
        named = jnp.where(first | second, 1.0, 0.0)
        before_of = lax.broadcasted_iota(jnp.int32, (tokens, tokens), 0) < lax.broadcasted_iota(jnp.int32, (tokens, tokens), 1)
        before = jnp.dot(named.astype(bf16), jnp.where(before_of, 1.0, 0.0).astype(bf16), preferred_element_type=f32)
        rank = jnp.where(named > 0.5, before, 255.0)
        spread = jnp.where(
            (lax.broadcasted_iota(jnp.int32, (half_rows, group), 0) // cap) == lax.broadcasted_iota(jnp.int32, (half_rows, group), 1), 1.0, 0.0
        ).astype(bf16)
        wide = jnp.dot(spread, rank.astype(bf16), preferred_element_type=f32)
        slot = lax.broadcasted_iota(jnp.int32, (half_rows, tokens), 0) & (cap - 1)
        return wide == slot.astype(f32), first, second, spread

    def route(meta_ref, token_ref, h):
        placed, _, _, _ = place(meta_ref, 1)
        rows = jnp.dot(jnp.where(placed, 1.0, 0.0).astype(bf16), token_ref[...], preferred_element_type=f32).astype(bf16)
        outb[h * half_rows:(h + 1) * half_rows, :] = rows
        gat[0, h * half_rows:h * half_rows + cap, :] = rows[0:cap]

    def rc(src, dst, ssem, rsem, device):
        return pltpu.make_async_remote_copy(src_ref=src, dst_ref=dst, send_sem=ssem, recv_sem=rsem, device_id=device, device_id_type=MESH)

    meta[0:2, :] = ids_ref[...]
    meta[2:4, :] = lev_ref[...]
    meta[4:8, :] = jnp.zeros((4, tokens), jnp.int32)
    gains[0] = jnp.broadcast_to(gain_ref[...].astype(f32), (16, quarter)).astype(bf16)
    route(meta, tok_ref, 0)

    pl.semaphore_wait(barrier, 2 * group + 2)

    nb = (z, across, d)
    to_right, to_left = (z, e, right), (z, e, left)
    copy_meta_nb = rc(meta, meta_nb, misc_s.at[0], misc_r.at[0], nb)
    copy_tok_nb = rc(tok_ref, tok_nb, misc_s.at[1], misc_r.at[1], nb)
    copy_meta_prev = rc(meta, meta_prev, misc_s.at[2], misc_r.at[2], (z_next, e, d))
    copy_tok_prev = rc(tok_ref, tok_prev, misc_s.at[3], misc_r.at[3], (z_next, e, d))
    copy_meta_pnb = rc(meta_prev, meta_pnb, misc_s.at[4], misc_r.at[4], nb)
    copy_gain_r = rc(gains.at[0], gains.at[1], misc_s.at[5], misc_r.at[5], to_right)
    copy_gain_l = rc(gains.at[0], gains.at[2], misc_s.at[6], misc_r.at[6], to_left)
    copy_gain_o = rc(gains.at[1], gains.at[3], misc_s.at[7], misc_r.at[7], to_right)
    copy_part = rc(xp_out, xp_in, misc_s.at[8], misc_r.at[8], nb)

    def dispatch(h, s):
        at = pl.ds(pl.multiple_of(h * half_rows + s * cap, cap), cap)
        return rc(outb.at[at, :], gat.at[0, at, :], disp_s.at[h, s], disp_r.at[h, s], (z, ahead(s), d))

    def giving_back(h, s):
        at = pl.ds(pl.multiple_of(h * half_rows + s * cap, cap), cap)
        return rc(res.at[at, :], ret.at[at, :], ret_s.at[h, s], ret_r.at[h, s], (z_next, behind(s), d))

    def each(low, high, action):
        def step(s, carry):
            action(s)
            return carry

        lax.fori_loop(low, high, step, 0)

    copy_meta_nb.start()
    copy_tok_nb.start()
    each(1, group, lambda s: dispatch(0, s).start())
    copy_gain_r.start()
    copy_gain_l.start()
    copy_meta_prev.start()

    chunks = [(0, 0), (1, 0), (1, group // 2), (0, group // 2)]
    starts = [h * half_rows + s * cap for h, s in chunks]

    def rows_of(c):
        return slice(starts[c], starts[c] + chunk)

    def upper(c):
        return slice(starts[c], starts[c] + split)

    def lower(c):
        return slice(starts[c] + split, starts[c] + chunk)

    def view(ref, q, at):
        return ref.at[q, pl.ds(at.start, at.stop - at.start), :]

    def flat(ref, at):
        return ref.at[pl.ds(at.start, at.stop - at.start), :]

    ag_r1 = [rc(view(gat, 0, rows_of(c)), view(gat, 1, rows_of(c)), ag_s.at[c, 0], ag_r.at[c, 0], to_right) for c in range(4)]
    ag_l1 = [rc(view(gat, 0, rows_of(c)), view(gat, 2, rows_of(c)), ag_s.at[c, 1], ag_r.at[c, 1], to_left) for c in range(4)]
    ag_r2 = [rc(view(gat, 1, upper(c)), view(gat, 3, upper(c)), ag_s.at[c, 2], ag_r.at[c, 2], to_right) for c in range(4)]
    ag_l2 = [rc(view(gat, 2, lower(c)), view(gat, 3, lower(c)), ag_s.at[c, 3], ag_r.at[c, 3], to_left) for c in range(4)]
    rs_r2 = [rc(view(part, 3, upper(c)), flat(rs_opp, upper(c)), rs_s.at[c, 0], rs_rr.at[c, 0], to_right) for c in range(4)]
    rs_l2 = [rc(view(part, 3, lower(c)), flat(rs_opp, lower(c)), rs_s.at[c, 1], rs_rr.at[c, 1], to_left) for c in range(4)]
    rs_r1 = [rc(view(part, 2, rows_of(c)), flat(rs_l, rows_of(c)), rs_s.at[c, 2], rs_rr.at[c, 2], to_right) for c in range(4)]
    rs_l1 = [rc(view(part, 1, rows_of(c)), flat(rs_r, rows_of(c)), rs_s.at[c, 3], rs_rr.at[c, 3], to_left) for c in range(4)]

    def gather(c):
        h, s0 = chunks[c]
        each(max(s0, 1), s0 + group // 2, lambda s: dispatch(h, s).wait_recv())
        ag_r1[c].start()
        ag_l1[c].start()

    def forward(c):
        ag_r1[c].wait_recv()
        ag_r2[c].start()
        ag_l1[c].wait_recv()
        ag_l2[c].start()

    def compute(c):
        at = rows_of(c)
        gate = jnp.zeros((chunk, wg.shape[2]), f32)
        up = jnp.zeros((chunk, wg.shape[2]), f32)
        squares = jnp.zeros((chunk, 1), f32)
        for q in range(4):
            if q == 3:
                ag_r2[c].wait_recv()
                ag_l2[c].wait_recv()
            wide = gat[q, at, :].astype(f32)
            squares = squares + jnp.sum(wide * wide, axis=1, keepdims=True)
            scaled = (wide * gains[q, 0:1, :].astype(f32)).astype(bf16)
            gate = gate + jnp.dot(scaled, wg[q], preferred_element_type=f32)
            up = up + jnp.dot(scaled, wu[q], preferred_element_type=f32)
        inverse = lax.rsqrt(squares / full_width + epsilon)
        gate = inverse * gate
        up = inverse * up
        hidden = (gate / (1.0 + jnp.exp(-gate)) * up).astype(bf16)
        part[3, at, :] = jnp.dot(hidden, wd[3], preferred_element_type=f32).astype(bf16)
        rs_r2[c].start()
        rs_l2[c].start()
        for q in (1, 2, 0):
            part[q, at, :] = jnp.dot(hidden, wd[q], preferred_element_type=f32).astype(bf16)

    def reduce_on(c):
        rs_r2[c].wait_recv()
        at = upper(c)
        part[2, at, :] = (part[2, at, :].astype(f32) + rs_opp[at, :].astype(f32)).astype(bf16)
        rs_r1[c].start()
        rs_l2[c].wait_recv()
        at = lower(c)
        part[1, at, :] = (part[1, at, :].astype(f32) + rs_opp[at, :].astype(f32)).astype(bf16)
        rs_l1[c].start()

    def give_back(c):
        at = rows_of(c)
        h, s0 = chunks[c]
        rs_r1[c].wait_recv()
        rs_l1[c].wait_recv()
        res[at, :] = (part[0, at, :].astype(f32) + rs_l[at, :].astype(f32) + rs_r[at, :].astype(f32)).astype(bf16)
        each(s0, s0 + group // 2, lambda s: giving_back(h, s).start())

    def combine(meta_ref, h):
        placed, first, second, spread = place(meta_ref, 1)
        levels = meta_ref[2:4, :].astype(f32)
        total = levels[0:1] + levels[1:2]
        share = jnp.where(first, levels[0:1] / total, jnp.where(second, levels[1:2] / total, 0.0))
        high = share.astype(bf16)
        low = (share - high.astype(f32)).astype(bf16)
        acc = jnp.zeros((tokens, quarter), f32)
        for piece in (high, low):
            weight = jnp.where(placed, jnp.dot(spread, piece, preferred_element_type=f32), 0.0).astype(bf16)
            acc = acc + lax.dot_general(
                weight, ret[h * half_rows:(h + 1) * half_rows, :], (((0,), (0,)), ((), ())), preferred_element_type=f32
            )
        return acc

    gather(0)
    copy_meta_nb.wait_recv()
    copy_tok_nb.wait_recv()
    route(meta_nb, tok_nb, 1)
    each(1, group, lambda s: dispatch(1, s).start())
    copy_tok_prev.start()
    gather(1)
    forward(0)
    copy_gain_r.wait_recv()
    copy_gain_o.start()
    gather(2)
    copy_meta_prev.wait_recv()
    copy_meta_pnb.start()
    gather(3)
    for copy in loads:
        copy.wait()
    copy_gain_l.wait_recv()
    copy_gain_o.wait_recv()
    compute(0)
    forward(1)
    reduce_on(0)
    compute(1)
    forward(2)
    give_back(0)
    reduce_on(1)
    compute(2)
    forward(3)
    give_back(1)
    reduce_on(2)
    compute(3)
    give_back(2)
    reduce_on(3)
    copy_meta_pnb.wait_recv()
    each(0, group, lambda s: giving_back(1, s).wait_recv())
    xp_out[...] = combine(meta_pnb, 1).astype(bf16)
    copy_part.start()
    give_back(3)
    copy_tok_prev.wait_recv()
    each(0, group, lambda s: giving_back(0, s).wait_recv())
    mine = combine(meta_prev, 0)
    copy_part.wait_recv()
    out_ref[...] = (tok_prev[...].astype(f32) + (mine + xp_in[...].astype(f32))).astype(bf16)

    for copy in (copy_meta_nb, copy_tok_nb, copy_meta_prev, copy_tok_prev, copy_meta_pnb, copy_gain_r, copy_gain_l, copy_gain_o, copy_part):
        copy.wait_send()
    for c in range(4):
        for copies in (ag_r1, ag_l1, ag_r2, ag_l2, rs_r2, rs_l2, rs_r1, rs_l1):
            copies[c].wait_send()
    for h in range(2):
        each(1, group, lambda s: dispatch(h, s).wait_send())
        each(0, group, lambda s: giving_back(h, s).wait_send())


def body(sizes, interpret, tokens, expert_ids, gate_levels, gain, w_gate, w_up, w_down):
    rows, quarter = tokens.shape[1:]
    fanout = expert_ids.shape[2]
    n_exp = sizes[1]
    cap = min(rows, max(2, 2 * rows * fanout // n_exp))
    group = n_exp // 2
    every = 2 * group * cap
    ff = w_gate.shape[2]
    vmem = pl.BlockSpec(memory_space=pltpu.VMEM)
    anywhere = pl.BlockSpec(memory_space=pl.ANY)
    dma = pltpu.SemaphoreType.DMA
    out = pl.pallas_call(
        functools.partial(kernel, sizes, cap),
        out_shape=jax.ShapeDtypeStruct((rows, quarter), bf16),
        in_specs=[vmem, vmem, vmem, vmem, anywhere, anywhere, anywhere],
        out_specs=vmem,
        scratch_shapes=[
            pltpu.VMEM((4, quarter, ff), bf16),
            pltpu.VMEM((4, quarter, ff), bf16),
            pltpu.VMEM((4, ff, quarter), bf16),
            *[pltpu.VMEM((8, rows), jnp.int32)] * 4,
            *[pltpu.VMEM((rows, quarter), bf16)] * 2,
            pltpu.VMEM((every, quarter), bf16),
            pltpu.VMEM((4, every, quarter), bf16),
            pltpu.VMEM((4, 16, quarter), bf16),
            pltpu.VMEM((4, every, quarter), bf16),
            *[pltpu.VMEM((every, quarter), bf16)] * 5,
            *[pltpu.VMEM((rows, quarter), bf16)] * 2,
            dma((12,)),
            dma((2, group)),
            dma((2, group)),
            dma((4, 4)),
            dma((4, 4)),
            dma((4, 4)),
            dma((4, 4)),
            dma((2, group)),
            dma((2, group)),
            dma((9,)),
            dma((9,)),
        ],
        compiler_params=pltpu.CompilerParams(collective_id=0, has_side_effects=True, vmem_limit_bytes=48 * 1024 * 1024),
        interpret=interpret,
    )(expert_ids[0].T, gate_levels[0].T, tokens[0], gain[None, :], w_gate[0], w_up[0], w_down[0])
    return out[None]


def solution(mesh, interpret=False):
    sizes = (mesh.shape["pipe"], mesh.shape["expert"], mesh.shape["dp"])
    return jax.shard_map(
        functools.partial(body, sizes, interpret),
        mesh=mesh,
        in_specs=(
            P("pipe", "expert", "dp"),
            P("pipe", "expert", None),
            P("pipe", "expert", None),
            P("dp"),
            P("expert", None, "dp"),
            P("expert", None, "dp"),
            P("expert", "dp", None),
        ),
        out_specs=P("pipe", "expert", "dp"),
        check_vma=False,
    )
```

```python
import functools

import jax
import jax.numpy as jnp
from jax import lax
from jax.experimental import pallas as pl
from jax.experimental.pallas import tpu as pltpu
from jax.sharding import PartitionSpec as P

MESH = pl.DeviceIdType.MESH
epsilon = 1e-06
bf16 = jnp.bfloat16
f32 = jnp.float32


def kernel(sizes, cap, ids_ref, lev_ref, tok_ref, gain_ref, wg_any, wu_any, wd_any, out_ref,
           wg, wu, wd, meta, meta_nb, meta_prev, meta_pnb, tok_nb, tok_prev, raw, onehot, outb, gat, gains,
           part, rs_opp, rs_l, rs_r, res, ret, cx_out, cx_in, xp_out, xp_in,
           w_sem, disp_s, disp_r, ag_s, ag_r, rs_s, rs_rr, ret_s, ret_r, misc_s, misc_r):
    n_pipe, n_exp, n_dp = sizes
    group = n_exp // 2
    tokens, quarter = tok_ref.shape
    half_rows = group * cap
    chunk = half_rows // 2
    split = chunk // 4
    full_width = n_dp * quarter

    z = lax.axis_index("pipe")
    e = lax.axis_index("expert")
    d = lax.axis_index("dp")
    x_lo = lax.rem(lax.div(e, 2), 2)
    g = lax.div(e, 4) * 2 + lax.rem(e, 2)
    right, left = lax.rem(d + 1, n_dp), lax.rem(d + n_dp - 1, n_dp)
    z_next, z_prev = lax.rem(z + 1, n_pipe), lax.rem(z + n_pipe - 1, n_pipe)

    def member(i):
        return lax.div(i, 2) * 4 + x_lo * 2 + lax.rem(i, 2)

    def offset(s):
        return jnp.where(lax.rem(s, 2) == 1, lax.div(s + 1, 2), group - lax.div(s, 2))

    def ahead(s):
        return member(lax.rem(g + offset(s), group))

    def behind(s):
        return member(lax.rem(g + 2 * group - offset(s), group))

    across = lax.div(e, 4) * 4 + (1 - x_lo) * 2 + lax.rem(e, 2)

    barrier = pltpu.get_barrier_semaphore()

    def tell_group(s, carry):
        pl.semaphore_signal(barrier, inc=1, device_id=(z, ahead(s), d), device_id_type=MESH)
        return carry

    def tell_before(s, carry):
        pl.semaphore_signal(barrier, inc=1, device_id=(z_prev, ahead(s), d), device_id_type=MESH)
        return carry

    pl.semaphore_signal(barrier, inc=1, device_id=(z, across, d), device_id_type=MESH)
    pl.semaphore_signal(barrier, inc=1, device_id=(z, across, right), device_id_type=MESH)
    pl.semaphore_signal(barrier, inc=1, device_id=(z, e, right), device_id_type=MESH)
    pl.semaphore_signal(barrier, inc=1, device_id=(z, e, left), device_id_type=MESH)
    lax.fori_loop(1, group, tell_group, 0)
    lax.fori_loop(0, group, tell_before, 0)

    quarters = [d, left, right, lax.rem(d + 2, n_dp)]
    loads = []
    for q in range(4):
        at = pl.ds(pl.multiple_of(quarters[q] * quarter, 128), quarter)
        loads.append(pltpu.make_async_copy(wg_any.at[at, :], wg.at[q], w_sem.at[3 * q]))
        loads.append(pltpu.make_async_copy(wu_any.at[at, :], wu.at[q], w_sem.at[3 * q + 1]))
        loads.append(pltpu.make_async_copy(wd_any.at[:, at], wd.at[q], w_sem.at[3 * q + 2]))
    for copy in loads:
        copy.start()

    def place(meta_ref):
        i = lax.broadcasted_iota(jnp.int32, (group, tokens), 0)
        off = jnp.where((i & 1) == 1, (i + 1) >> 1, group - (i >> 1))
        member_of = (g + off) & (group - 1)
        expert = (member_of >> 1) * 4 + x_lo * 2 + (member_of & 1)
        first = meta_ref[0:1, :] == expert
        second = meta_ref[1:2, :] == expert
        named = jnp.where(first | second, 1.0, 0.0)
        earlier = lax.broadcasted_iota(jnp.int32, (tokens, tokens), 0) < lax.broadcasted_iota(jnp.int32, (tokens, tokens), 1)
        before = jnp.dot(named.astype(bf16), jnp.where(earlier, 1.0, 0.0).astype(bf16), preferred_element_type=f32)
        rank = jnp.where(named > 0.5, before, 255.0)
        owner = lax.broadcasted_iota(jnp.int32, (half_rows, group), 0) // cap
        spread = jnp.where(owner == lax.broadcasted_iota(jnp.int32, (half_rows, group), 1), 1.0, 0.0).astype(bf16)
        wide = jnp.dot(spread, rank.astype(bf16), preferred_element_type=f32)
        slot = lax.broadcasted_iota(jnp.int32, (half_rows, tokens), 0) & (cap - 1)
        return wide == slot.astype(f32), first, second, spread

    extra, other = (1, 2), (2, 1)

    def kept(h, k):
        return extra[h] if k else 0

    def rc(src, dst, ssem, rsem, device):
        return pltpu.make_async_remote_copy(src_ref=src, dst_ref=dst, send_sem=ssem, recv_sem=rsem, device_id=device, device_id_type=MESH)

    def each(low, high, action):
        def step(s, carry):
            action(s)
            return carry

        lax.fori_loop(low, high, step, 0)

    def route(h, k, token_ref):
        rows = jnp.dot(onehot[h], token_ref[...], preferred_element_type=f32).astype(bf16)
        outb[k, h * half_rows:(h + 1) * half_rows, :] = rows
        gat[kept(h, k), h * half_rows:h * half_rows + cap, :] = rows[0:cap]

    meta[0:2, :] = ids_ref[...]
    meta[2:4, :] = lev_ref[...]
    meta[4:8, :] = jnp.zeros((4, tokens), jnp.int32)
    gains[0] = jnp.broadcast_to(gain_ref[...].astype(f32).reshape(1, quarter), (16, quarter)).astype(bf16)
    onehot[0] = jnp.where(place(meta)[0], 1.0, 0.0).astype(bf16)
    route(0, 0, tok_ref)

    pl.semaphore_wait(barrier, 2 * group + 3)

    nb = (z, across, d)
    to_right, to_left = (z, e, right), (z, e, left)
    to = (None, to_left, to_right)
    copy_meta_nb = rc(meta, meta_nb, misc_s.at[0], misc_r.at[0], nb)
    copy_tok_nb = rc(tok_ref, tok_nb, misc_s.at[1], misc_r.at[1], nb)
    copy_meta_prev = rc(meta, meta_prev, misc_s.at[2], misc_r.at[2], (z_next, e, d))
    copy_tok_prev = rc(tok_ref, tok_prev, misc_s.at[3], misc_r.at[3], (z_next, e, d))
    copy_meta_pnb = rc(meta_prev, meta_pnb, misc_s.at[4], misc_r.at[4], nb)
    copy_gain_r = rc(gains.at[0], gains.at[1], misc_s.at[5], misc_r.at[5], to_right)
    copy_gain_l = rc(gains.at[0], gains.at[2], misc_s.at[6], misc_r.at[6], to_left)
    copy_gain_o = rc(gains.at[1], gains.at[3], misc_s.at[7], misc_r.at[7], to_right)
    copy_part = rc(xp_out, xp_in, misc_s.at[8], misc_r.at[8], nb)
    copy_raw = [rc(tok_ref, raw.at[h], misc_s.at[9 + h], misc_r.at[9 + h], there) for h, there in enumerate((to_right, (z, across, left)))]
    copy_cx = rc(cx_out, cx_in, misc_s.at[11], misc_r.at[11], to[extra[1]])

    def dispatch(h, k, s):
        at = pl.ds(pl.multiple_of(h * half_rows + s * cap, cap), cap)
        sem = (2 * h + k, s)
        return rc(outb.at[k, at, :], gat.at[kept(h, k), at, :], disp_s.at[sem], disp_r.at[sem], (z, ahead(s), d))

    def giving_back(h, k, s):
        at = pl.ds(pl.multiple_of(h * half_rows + s * cap, cap), cap)
        sem = (2 * h + k, s)
        return rc(res.at[k, at, :], ret.at[k, at, :], ret_s.at[sem], ret_r.at[sem], (z_next, behind(s), d))

    chunks = [(0, 0), (1, 0), (1, 1), (0, 1)]
    C00, C10, C11, C01 = 0, 1, 2, 3
    starts = [h * half_rows + p * chunk for h, p in chunks]

    def rows_of(c):
        return pl.ds(starts[c], chunk)

    def upper(c):
        return pl.ds(starts[c], split)

    def lower(c):
        return pl.ds(starts[c] + split, chunk - split)

    def send_rows(c, k):
        h, p = chunks[c]
        each(max(p * (group // 2), 1), (p + 1) * (group // 2), lambda s: dispatch(h, k, s).start())

    def wait_rows(c, k):
        h, p = chunks[c]
        each(max(p * (group // 2), 1), (p + 1) * (group // 2), lambda s: dispatch(h, k, s).wait_recv())

    ag = [
        [
            rc(gat.at[0, rows_of(c), :], gat.at[other[h], rows_of(c), :], ag_s.at[c, 0], ag_r.at[c, 0], to[extra[h]]),
            rc(gat.at[extra[h], rows_of(c), :], gat.at[3, rows_of(c), :], ag_s.at[c, 1], ag_r.at[c, 1], to[other[h]]),
        ]
        for c, (h, _) in enumerate(chunks)
    ]

    def ring(c):
        return chunks[c][0] == 0

    rs = []
    for c, (h, _) in enumerate(chunks):
        if ring(c):
            rs.append([
                rc(part.at[3, upper(c), :], rs_opp.at[upper(c), :], rs_s.at[c, 0], rs_rr.at[c, 0], to_right),
                rc(part.at[3, lower(c), :], rs_opp.at[lower(c), :], rs_s.at[c, 1], rs_rr.at[c, 1], to_left),
                rc(part.at[2, rows_of(c), :], rs_l.at[rows_of(c), :], rs_s.at[c, 2], rs_rr.at[c, 2], to_right),
                rc(part.at[1, rows_of(c), :], rs_r.at[rows_of(c), :], rs_s.at[c, 3], rs_rr.at[c, 3], to_left),
            ])
        else:
            rs.append([
                rc(part.at[3, rows_of(c), :], rs_l.at[rows_of(c), :], rs_s.at[c, 0], rs_rr.at[c, 0], to[extra[h]]),
                rc(part.at[other[h], rows_of(c), :], rs_r.at[rows_of(c), :], rs_s.at[c, 1], rs_rr.at[c, 1], to[other[h]]),
            ])

    def compute(c):
        h, _ = chunks[c]
        at = rows_of(c)
        gate = jnp.zeros((chunk, wg.shape[2]), f32)
        up = jnp.zeros((chunk, wg.shape[2]), f32)
        squares = jnp.zeros((chunk, 1), f32)
        for q in (0, extra[h], other[h], 3):
            if q == other[h]:
                ag[c][0].wait_recv()
            if q == 3:
                ag[c][1].wait_recv()
            wide = gat[q, at, :].astype(f32)
            squares = squares + jnp.sum(wide * wide, axis=1, keepdims=True)
            scaled = (wide * gains[q, 0:1, :].astype(f32)).astype(bf16)
            gate = gate + jnp.dot(scaled, wg[q], preferred_element_type=f32)
            up = up + jnp.dot(scaled, wu[q], preferred_element_type=f32)
        inverse = lax.rsqrt(squares / full_width + epsilon)
        gate = inverse * gate
        up = inverse * up
        hidden = (gate / (1.0 + jnp.exp(-gate)) * up).astype(bf16)
        for q in (3, other[h], extra[h], 0):
            part[q, at, :] = jnp.dot(hidden, wd[q], preferred_element_type=f32).astype(bf16)
            if q == 3:
                rs[c][0].start()
                if ring(c):
                    rs[c][1].start()
            if q == other[h] and not ring(c):
                rs[c][1].start()

    def reduce_on(c):
        rs[c][0].wait_recv()
        at = upper(c)
        part[2, at, :] = (part[2, at, :].astype(f32) + rs_opp[at, :].astype(f32)).astype(bf16)
        rs[c][2].start()
        rs[c][1].wait_recv()
        at = lower(c)
        part[1, at, :] = (part[1, at, :].astype(f32) + rs_opp[at, :].astype(f32)).astype(bf16)
        rs[c][3].start()

    def give_back(c, k):
        h, p = chunks[c]
        at = rows_of(c)
        if ring(c):
            rs[c][2].wait_recv()
            rs[c][3].wait_recv()
            total = part[0, at, :].astype(f32) + rs_l[at, :].astype(f32) + rs_r[at, :].astype(f32)
        elif k:
            rs[c][0].wait_recv()
            total = part[extra[h], at, :].astype(f32) + rs_l[at, :].astype(f32)
        else:
            rs[c][1].wait_recv()
            total = part[0, at, :].astype(f32) + rs_r[at, :].astype(f32)
        res[k, at, :] = total.astype(bf16)
        each(p * (group // 2), (p + 1) * (group // 2), lambda s: giving_back(h, k, s).start())

    def weights(meta_ref):
        placed, first, second, spread = place(meta_ref)
        levels = meta_ref[2:4, :].astype(f32)
        total = levels[0:1] + levels[1:2]
        share = jnp.where(first, levels[0:1] / total, jnp.where(second, levels[1:2] / total, 0.0))
        high = share.astype(bf16)
        low = (share - high.astype(f32)).astype(bf16)
        return [jnp.where(placed, jnp.dot(spread, piece, preferred_element_type=f32), 0.0).astype(bf16) for piece in (high, low)]

    def combine(pieces, h, k):
        each(0, group, lambda s: giving_back(h, k, s).wait_recv())
        acc = jnp.zeros((tokens, quarter), f32)
        for piece in pieces:
            acc = acc + lax.dot_general(
                piece, ret[k, h * half_rows:(h + 1) * half_rows, :], (((0,), (0,)), ((), ())), preferred_element_type=f32
            )
        return acc

    copy_meta_nb.start()
    copy_tok_nb.start()
    copy_raw[0].start()
    copy_raw[1].start()
    send_rows(C00, 0)
    copy_gain_r.start()
    copy_gain_l.start()
    copy_meta_prev.start()
    copy_meta_nb.wait_recv()
    onehot[1] = jnp.where(place(meta_nb)[0], 1.0, 0.0).astype(bf16)
    copy_tok_nb.wait_recv()
    route(1, 0, tok_nb)
    send_rows(C10, 0)
    wait_rows(C00, 0)
    ag[C00][0].start()
    copy_raw[0].wait_recv()
    route(0, 1, raw.at[0])
    send_rows(C00, 1)
    copy_raw[1].wait_recv()
    route(1, 1, raw.at[1])
    send_rows(C10, 1)
    send_rows(C01, 0)
    send_rows(C11, 0)
    send_rows(C01, 1)
    send_rows(C11, 1)
    wait_rows(C10, 0)
    ag[C10][0].start()
    copy_gain_r.wait_recv()
    copy_gain_o.start()
    wait_rows(C00, 1)
    ag[C00][1].start()
    wait_rows(C10, 1)
    ag[C10][1].start()
    copy_meta_prev.wait_recv()
    copy_meta_pnb.start()
    for copy in loads:
        copy.wait()
    copy_gain_l.wait_recv()
    copy_gain_o.wait_recv()
    wait_rows(C01, 0)
    ag[C01][0].start()
    wait_rows(C11, 0)
    ag[C11][0].start()
    compute(C00)
    wait_rows(C01, 1)
    ag[C01][1].start()
    compute(C10)
    wait_rows(C11, 1)
    ag[C11][1].start()
    copy_tok_prev.start()
    reduce_on(C00)
    copy_meta_pnb.wait_recv()
    compute(C11)
    compute(C01)
    give_back(C10, 1)
    give_back(C10, 0)
    give_back(C00, 0)
    give_back(C11, 1)
    give_back(C11, 0)
    reduce_on(C01)
    pieces = weights(meta_pnb)
    cx_out[...] = combine(pieces, 1, 1).astype(bf16)
    copy_cx.start()
    theirs = combine(pieces, 1, 0)
    give_back(C01, 0)
    copy_cx.wait_recv()
    xp_out[...] = (theirs + cx_in[...].astype(f32)).astype(bf16)
    copy_part.start()
    copy_tok_prev.wait_recv()
    mine = combine(weights(meta_prev), 0, 0)
    copy_part.wait_recv()
    out_ref[...] = (tok_prev[...].astype(f32) + (mine + xp_in[...].astype(f32))).astype(bf16)

    for copy in (copy_meta_nb, copy_tok_nb, copy_meta_prev, copy_tok_prev, copy_meta_pnb, copy_gain_r, copy_gain_l, copy_gain_o, copy_part, copy_cx, *copy_raw):
        copy.wait_send()
    for c in range(4):
        for copy in (*ag[c], *rs[c]):
            copy.wait_send()
    for h in range(2):
        for k in range(2):
            each(1, group, lambda s: dispatch(h, k, s).wait_send())
            if k == 0 or h == 1:
                each(0, group, lambda s: giving_back(h, k, s).wait_send())


def body(sizes, interpret, tokens, expert_ids, gate_levels, gain, w_gate, w_up, w_down):
    rows, quarter = tokens.shape[1:]
    fanout = expert_ids.shape[2]
    n_exp = sizes[1]
    cap = min(rows, max(2, 2 * rows * fanout // n_exp))
    group = n_exp // 2
    every = 2 * group * cap
    ff = w_gate.shape[2]
    vmem = pl.BlockSpec(memory_space=pltpu.VMEM)
    anywhere = pl.BlockSpec(memory_space=pl.ANY)
    dma = pltpu.SemaphoreType.DMA
    out = pl.pallas_call(
        functools.partial(kernel, sizes, cap),
        out_shape=jax.ShapeDtypeStruct((rows, quarter), bf16),
        in_specs=[vmem, vmem, vmem, vmem, anywhere, anywhere, anywhere],
        out_specs=vmem,
        scratch_shapes=[
            pltpu.VMEM((4, quarter, ff), bf16),
            pltpu.VMEM((4, quarter, ff), bf16),
            pltpu.VMEM((4, ff, quarter), bf16),
            *[pltpu.VMEM((8, rows), jnp.int32)] * 4,
            *[pltpu.VMEM((rows, quarter), bf16)] * 2,
            pltpu.VMEM((2, rows, quarter), bf16),
            pltpu.VMEM((2, group * cap, rows), bf16),
            pltpu.VMEM((2, every, quarter), bf16),
            pltpu.VMEM((4, every, quarter), bf16),
            pltpu.VMEM((4, 16, quarter), bf16),
            pltpu.VMEM((4, every, quarter), bf16),
            *[pltpu.VMEM((every, quarter), bf16)] * 3,
            *[pltpu.VMEM((2, every, quarter), bf16)] * 2,
            *[pltpu.VMEM((rows, quarter), bf16)] * 4,
            dma((12,)),
            dma((4, group)),
            dma((4, group)),
            *[dma((4, 2))] * 2,
            *[dma((4, 4))] * 2,
            dma((4, group)),
            dma((4, group)),
            dma((12,)),
            dma((12,)),
        ],
        compiler_params=pltpu.CompilerParams(collective_id=0, has_side_effects=True, vmem_limit_bytes=61 * 1024 * 1024),
        interpret=interpret,
    )(expert_ids[0].T, gate_levels[0].T, tokens[0], gain, w_gate[0], w_up[0], w_down[0])
    return out[None]


def solution(mesh, interpret=False):
    sizes = (mesh.shape["pipe"], mesh.shape["expert"], mesh.shape["dp"])
    return jax.shard_map(
        functools.partial(body, sizes, interpret),
        mesh=mesh,
        in_specs=(
            P("pipe", "expert", "dp"),
            P("pipe", "expert", None),
            P("pipe", "expert", None),
            P("dp"),
            P("expert", None, "dp"),
            P("expert", None, "dp"),
            P("expert", "dp", None),
        ),
        out_specs=P("pipe", "expert", "dp"),
        check_vma=False,
    )
```

```python
import functools

import jax
import jax.numpy as jnp
from jax import lax
from jax.experimental import pallas as pl
from jax.experimental.pallas import tpu as pltpu
from jax.sharding import PartitionSpec as P

MESH = pl.DeviceIdType.MESH
epsilon = 1e-06
bf16 = jnp.bfloat16
f32 = jnp.float32


def kernel(sizes, cap, ids_ref, lev_ref, tok_ref, gain_ref, wg_any, wu_any, wd_any, out_ref,
           wg, wu, wd, meta, meta_nb, meta_prev, meta_pnb, tok_nb, tok_prev, raw, onehot, shares, outb, gat, gains,
           part, rs_opp, rs_l, rs_r, res, ret, cx_out, cx_in, xp_out, xp_in,
           w_sem, disp_s, disp_r, ag_s, ag_r, rs_s, rs_rr, ret_s, ret_r, misc_s, misc_r):
    n_pipe, n_exp, n_dp = sizes
    group = n_exp // 2
    tokens, quarter = tok_ref.shape
    half_rows = group * cap
    chunk = half_rows // 2
    split = chunk // 4
    full_width = n_dp * quarter

    z = lax.axis_index("pipe")
    e = lax.axis_index("expert")
    d = lax.axis_index("dp")
    x_lo = lax.rem(lax.div(e, 2), 2)
    g = lax.div(e, 4) * 2 + lax.rem(e, 2)
    right, left = lax.rem(d + 1, n_dp), lax.rem(d + n_dp - 1, n_dp)
    z_next, z_prev = lax.rem(z + 1, n_pipe), lax.rem(z + n_pipe - 1, n_pipe)

    def member(i):
        return lax.div(i, 2) * 4 + x_lo * 2 + lax.rem(i, 2)

    def offset(s):
        return jnp.where(lax.rem(s, 2) == 1, lax.div(s + 1, 2), group - lax.div(s, 2))

    def ahead(s):
        return member(lax.rem(g + offset(s), group))

    def behind(s):
        return member(lax.rem(g + 2 * group - offset(s), group))

    across = lax.div(e, 4) * 4 + (1 - x_lo) * 2 + lax.rem(e, 2)

    barrier = pltpu.get_barrier_semaphore()

    def tell_group(s, carry):
        pl.semaphore_signal(barrier, inc=1, device_id=(z, ahead(s), d), device_id_type=MESH)
        return carry

    def tell_before(s, carry):
        pl.semaphore_signal(barrier, inc=1, device_id=(z_prev, ahead(s), d), device_id_type=MESH)
        return carry

    pl.semaphore_signal(barrier, inc=1, device_id=(z, across, d), device_id_type=MESH)
    pl.semaphore_signal(barrier, inc=1, device_id=(z, across, right), device_id_type=MESH)
    pl.semaphore_signal(barrier, inc=1, device_id=(z, e, right), device_id_type=MESH)
    pl.semaphore_signal(barrier, inc=1, device_id=(z, e, left), device_id_type=MESH)
    lax.fori_loop(1, group, tell_group, 0)
    lax.fori_loop(0, group, tell_before, 0)

    quarters = [d, left, right, lax.rem(d + 2, n_dp)]
    loads = []
    for q in range(4):
        at = pl.ds(pl.multiple_of(quarters[q] * quarter, 128), quarter)
        loads.append(pltpu.make_async_copy(wg_any.at[at, :], wg.at[q], w_sem.at[3 * q]))
        loads.append(pltpu.make_async_copy(wu_any.at[at, :], wu.at[q], w_sem.at[3 * q + 1]))
        loads.append(pltpu.make_async_copy(wd_any.at[:, at], wd.at[q], w_sem.at[3 * q + 2]))
    for copy in loads:
        copy.start()

    def place(meta_ref):
        i = lax.broadcasted_iota(jnp.int32, (group, tokens), 0)
        off = jnp.where((i & 1) == 1, (i + 1) >> 1, group - (i >> 1))
        member_of = (g + off) & (group - 1)
        expert = (member_of >> 1) * 4 + x_lo * 2 + (member_of & 1)
        first = meta_ref[0:1, :] == expert
        second = meta_ref[1:2, :] == expert
        named = jnp.where(first | second, 1.0, 0.0)
        earlier = lax.broadcasted_iota(jnp.int32, (tokens, tokens), 0) < lax.broadcasted_iota(jnp.int32, (tokens, tokens), 1)
        before = jnp.dot(named.astype(bf16), jnp.where(earlier, 1.0, 0.0).astype(bf16), preferred_element_type=f32)
        rank = jnp.where(named > 0.5, before, 255.0)
        owner = lax.broadcasted_iota(jnp.int32, (half_rows, group), 0) // cap
        spread = jnp.where(owner == lax.broadcasted_iota(jnp.int32, (half_rows, group), 1), 1.0, 0.0).astype(bf16)
        wide = jnp.dot(spread, rank.astype(bf16), preferred_element_type=f32)
        slot = lax.broadcasted_iota(jnp.int32, (half_rows, tokens), 0) & (cap - 1)
        return wide == slot.astype(f32), first, second, spread

    extra, other = (1, 2), (2, 1)

    def kept(h, k):
        return extra[h] if k else 0

    def rc(src, dst, ssem, rsem, device):
        return pltpu.make_async_remote_copy(src_ref=src, dst_ref=dst, send_sem=ssem, recv_sem=rsem, device_id=device, device_id_type=MESH)

    def each(low, high, action):
        def step(s, carry):
            action(s)
            return carry

        lax.fori_loop(low, high, step, 0)

    def route(h, k, token_ref):
        rows = jnp.dot(onehot[h], token_ref[...], preferred_element_type=f32).astype(bf16)
        outb[k, h * half_rows:(h + 1) * half_rows, :] = rows
        gat[kept(h, k), h * half_rows:h * half_rows + cap, :] = rows[0:cap]

    meta[0:2, :] = ids_ref[...]
    meta[2:4, :] = lev_ref[...]
    meta[4:8, :] = jnp.zeros((4, tokens), jnp.int32)
    gains[0] = jnp.broadcast_to(gain_ref[...].astype(f32).reshape(1, quarter), (16, quarter)).astype(bf16)
    onehot[0] = jnp.where(place(meta)[0], 1.0, 0.0).astype(bf16)
    route(0, 0, tok_ref)

    pl.semaphore_wait(barrier, 2 * group + 3)

    nb = (z, across, d)
    to_right, to_left = (z, e, right), (z, e, left)
    to = (None, to_left, to_right)
    copy_meta_nb = rc(meta, meta_nb, misc_s.at[0], misc_r.at[0], nb)
    copy_tok_nb = rc(tok_ref, tok_nb, misc_s.at[1], misc_r.at[1], nb)
    copy_meta_prev = rc(meta, meta_prev, misc_s.at[2], misc_r.at[2], (z_next, e, d))
    copy_tok_prev = rc(tok_ref, tok_prev, misc_s.at[3], misc_r.at[3], (z_next, e, d))
    copy_meta_pnb = rc(meta_prev, meta_pnb, misc_s.at[4], misc_r.at[4], nb)
    copy_gain_r = rc(gains.at[0], gains.at[1], misc_s.at[5], misc_r.at[5], to_right)
    copy_gain_l = rc(gains.at[0], gains.at[2], misc_s.at[6], misc_r.at[6], to_left)
    copy_gain_o = rc(gains.at[1], gains.at[3], misc_s.at[7], misc_r.at[7], to_right)
    copy_part = rc(xp_out, xp_in, misc_s.at[8], misc_r.at[8], nb)
    copy_raw = [rc(tok_ref, raw.at[h], misc_s.at[9 + h], misc_r.at[9 + h], there) for h, there in enumerate((to_right, (z, across, left)))]
    copy_cx = rc(cx_out, cx_in, misc_s.at[11], misc_r.at[11], to[extra[1]])

    def dispatch(h, k, s):
        at = pl.ds(pl.multiple_of(h * half_rows + s * cap, cap), cap)
        sem = (2 * h + k, s)
        return rc(outb.at[k, at, :], gat.at[kept(h, k), at, :], disp_s.at[sem], disp_r.at[sem], (z, ahead(s), d))

    def giving_back(h, k, s):
        at = pl.ds(pl.multiple_of(h * half_rows + s * cap, cap), cap)
        sem = (2 * h + k, s)
        return rc(res.at[k, at, :], ret.at[k, at, :], ret_s.at[sem], ret_r.at[sem], (z_next, behind(s), d))

    chunks = [(0, 0), (1, 0), (1, 1), (0, 1)]
    C00, C10, C11, C01 = 0, 1, 2, 3
    starts = [h * half_rows + p * chunk for h, p in chunks]

    def rows_of(c):
        return pl.ds(starts[c], chunk)

    def upper(c):
        return pl.ds(starts[c], split)

    def lower(c):
        return pl.ds(starts[c] + split, chunk - split)

    def send_rows(c, k):
        h, p = chunks[c]
        each(max(p * (group // 2), 1), (p + 1) * (group // 2), lambda s: dispatch(h, k, s).start())

    def wait_rows(c, k):
        h, p = chunks[c]
        each(max(p * (group // 2), 1), (p + 1) * (group // 2), lambda s: dispatch(h, k, s).wait_recv())

    ag = [
        [
            rc(gat.at[0, rows_of(c), :], gat.at[other[h], rows_of(c), :], ag_s.at[c, 0], ag_r.at[c, 0], to[extra[h]]),
            rc(gat.at[extra[h], rows_of(c), :], gat.at[3, rows_of(c), :], ag_s.at[c, 1], ag_r.at[c, 1], to[other[h]]),
        ]
        for c, (h, _) in enumerate(chunks)
    ]

    def ring(c):
        return chunks[c][0] == 0

    rs = []
    for c, (h, _) in enumerate(chunks):
        if ring(c):
            rs.append([
                rc(part.at[3, upper(c), :], rs_opp.at[upper(c), :], rs_s.at[c, 0], rs_rr.at[c, 0], to_right),
                rc(part.at[3, lower(c), :], rs_opp.at[lower(c), :], rs_s.at[c, 1], rs_rr.at[c, 1], to_left),
                rc(part.at[2, rows_of(c), :], rs_l.at[rows_of(c), :], rs_s.at[c, 2], rs_rr.at[c, 2], to_right),
                rc(part.at[1, rows_of(c), :], rs_r.at[rows_of(c), :], rs_s.at[c, 3], rs_rr.at[c, 3], to_left),
            ])
        else:
            rs.append([
                rc(part.at[3, rows_of(c), :], rs_l.at[rows_of(c), :], rs_s.at[c, 0], rs_rr.at[c, 0], to[extra[h]]),
                rc(part.at[other[h], rows_of(c), :], rs_r.at[rows_of(c), :], rs_s.at[c, 1], rs_rr.at[c, 1], to[other[h]]),
            ])

    def compute(c):
        h, _ = chunks[c]
        at = rows_of(c)
        gate = jnp.zeros((chunk, wg.shape[2]), f32)
        up = jnp.zeros((chunk, wg.shape[2]), f32)
        squares = jnp.zeros((chunk, 1), f32)
        for q in (0, extra[h], other[h], 3):
            if q == other[h]:
                ag[c][0].wait_recv()
            if q == 3:
                ag[c][1].wait_recv()
            wide = gat[q, at, :].astype(f32)
            squares = squares + jnp.sum(wide * wide, axis=1, keepdims=True)
            scaled = (wide * gains[q, 0:1, :].astype(f32)).astype(bf16)
            gate = gate + jnp.dot(scaled, wg[q], preferred_element_type=f32)
            up = up + jnp.dot(scaled, wu[q], preferred_element_type=f32)
        inverse = lax.rsqrt(squares / full_width + epsilon)
        gate = inverse * gate
        up = inverse * up
        hidden = (gate / (1.0 + jnp.exp(-gate)) * up).astype(bf16)
        for q in (3, other[h], extra[h], 0):
            part[q, at, :] = jnp.dot(hidden, wd[q], preferred_element_type=f32).astype(bf16)
            if q == 3:
                rs[c][0].start()
                if ring(c):
                    rs[c][1].start()
            if q == other[h] and not ring(c):
                rs[c][1].start()

    def reduce_on(c):
        rs[c][0].wait_recv()
        at = upper(c)
        part[2, at, :] = (part[2, at, :].astype(f32) + rs_opp[at, :].astype(f32)).astype(bf16)
        rs[c][2].start()
        rs[c][1].wait_recv()
        at = lower(c)
        part[1, at, :] = (part[1, at, :].astype(f32) + rs_opp[at, :].astype(f32)).astype(bf16)
        rs[c][3].start()

    def give_back(c, k):
        h, p = chunks[c]
        at = rows_of(c)
        if ring(c):
            rs[c][2].wait_recv()
            rs[c][3].wait_recv()
            total = part[0, at, :].astype(f32) + rs_l[at, :].astype(f32) + rs_r[at, :].astype(f32)
        elif k:
            rs[c][0].wait_recv()
            total = part[extra[h], at, :].astype(f32) + rs_l[at, :].astype(f32)
        else:
            rs[c][1].wait_recv()
            total = part[0, at, :].astype(f32) + rs_r[at, :].astype(f32)
        res[k, at, :] = total.astype(bf16)
        each(p * (group // 2), (p + 1) * (group // 2), lambda s: giving_back(h, k, s).start())

    def share(meta_ref, h):
        placed, first, second, spread = place(meta_ref)
        levels = meta_ref[2:4, :].astype(f32)
        total = levels[0:1] + levels[1:2]
        part_of = jnp.where(first, levels[0:1] / total, jnp.where(second, levels[1:2] / total, 0.0))
        high = part_of.astype(bf16)
        low = (part_of - high.astype(f32)).astype(bf16)
        for i, term in enumerate((high, low)):
            shares[2 * h + i] = jnp.where(placed, jnp.dot(spread, term, preferred_element_type=f32), 0.0).astype(bf16)

    def combine(h, k):
        each(0, group, lambda s: giving_back(h, k, s).wait_recv())
        acc = jnp.zeros((tokens, quarter), f32)
        for i in range(2):
            acc = acc + lax.dot_general(
                shares[2 * h + i], ret[k, h * half_rows:(h + 1) * half_rows, :], (((0,), (0,)), ((), ())), preferred_element_type=f32
            )
        return acc

    copy_meta_nb.start()
    copy_tok_nb.start()
    copy_raw[0].start()
    copy_raw[1].start()
    send_rows(C00, 0)
    copy_gain_r.start()
    copy_gain_l.start()
    copy_meta_prev.start()
    copy_meta_nb.wait_recv()
    onehot[1] = jnp.where(place(meta_nb)[0], 1.0, 0.0).astype(bf16)
    copy_tok_nb.wait_recv()
    route(1, 0, tok_nb)
    send_rows(C10, 0)
    wait_rows(C00, 0)
    ag[C00][0].start()
    copy_raw[0].wait_recv()
    route(0, 1, raw.at[0])
    send_rows(C00, 1)
    copy_raw[1].wait_recv()
    route(1, 1, raw.at[1])
    send_rows(C10, 1)
    send_rows(C01, 0)
    send_rows(C11, 0)
    send_rows(C01, 1)
    send_rows(C11, 1)
    wait_rows(C10, 0)
    ag[C10][0].start()
    copy_gain_r.wait_recv()
    copy_gain_o.start()
    wait_rows(C00, 1)
    ag[C00][1].start()
    wait_rows(C10, 1)
    ag[C10][1].start()
    copy_meta_prev.wait_recv()
    copy_meta_pnb.start()
    for copy in loads:
        copy.wait()
    copy_gain_l.wait_recv()
    copy_gain_o.wait_recv()
    wait_rows(C01, 0)
    ag[C01][0].start()
    wait_rows(C11, 0)
    ag[C11][0].start()
    compute(C00)
    wait_rows(C01, 1)
    ag[C01][1].start()
    compute(C10)
    wait_rows(C11, 1)
    ag[C11][1].start()
    copy_tok_prev.start()
    reduce_on(C00)
    compute(C11)
    give_back(C10, 1)
    give_back(C10, 0)
    compute(C01)
    share(meta_prev, 0)
    copy_meta_pnb.wait_recv()
    share(meta_pnb, 1)
    give_back(C00, 0)
    give_back(C11, 1)
    reduce_on(C01)
    give_back(C11, 0)
    give_back(C01, 0)
    cx_out[...] = combine(1, 1).astype(bf16)
    copy_cx.start()
    theirs = combine(1, 0)
    copy_cx.wait_recv()
    xp_out[...] = (theirs + cx_in[...].astype(f32)).astype(bf16)
    copy_part.start()
    copy_tok_prev.wait_recv()
    mine = combine(0, 0)
    copy_part.wait_recv()
    out_ref[...] = (tok_prev[...].astype(f32) + (mine + xp_in[...].astype(f32))).astype(bf16)

    for copy in (copy_meta_nb, copy_tok_nb, copy_meta_prev, copy_tok_prev, copy_meta_pnb, copy_gain_r, copy_gain_l, copy_gain_o, copy_part, copy_cx, *copy_raw):
        copy.wait_send()
    for c in range(4):
        for copy in (*ag[c], *rs[c]):
            copy.wait_send()
    for h in range(2):
        for k in range(2):
            each(1, group, lambda s: dispatch(h, k, s).wait_send())
            if k == 0 or h == 1:
                each(0, group, lambda s: giving_back(h, k, s).wait_send())


def body(sizes, interpret, tokens, expert_ids, gate_levels, gain, w_gate, w_up, w_down):
    rows, quarter = tokens.shape[1:]
    fanout = expert_ids.shape[2]
    n_exp = sizes[1]
    cap = min(rows, max(2, 2 * rows * fanout // n_exp))
    group = n_exp // 2
    every = 2 * group * cap
    ff = w_gate.shape[2]
    vmem = pl.BlockSpec(memory_space=pltpu.VMEM)
    anywhere = pl.BlockSpec(memory_space=pl.ANY)
    dma = pltpu.SemaphoreType.DMA
    out = pl.pallas_call(
        functools.partial(kernel, sizes, cap),
        out_shape=jax.ShapeDtypeStruct((rows, quarter), bf16),
        in_specs=[vmem, vmem, vmem, vmem, anywhere, anywhere, anywhere],
        out_specs=vmem,
        scratch_shapes=[
            pltpu.VMEM((4, quarter, ff), bf16),
            pltpu.VMEM((4, quarter, ff), bf16),
            pltpu.VMEM((4, ff, quarter), bf16),
            *[pltpu.VMEM((8, rows), jnp.int32)] * 4,
            *[pltpu.VMEM((rows, quarter), bf16)] * 2,
            pltpu.VMEM((2, rows, quarter), bf16),
            pltpu.VMEM((2, group * cap, rows), bf16),
            pltpu.VMEM((4, group * cap, rows), bf16),
            pltpu.VMEM((2, every, quarter), bf16),
            pltpu.VMEM((4, every, quarter), bf16),
            pltpu.VMEM((4, 16, quarter), bf16),
            pltpu.VMEM((4, every, quarter), bf16),
            *[pltpu.VMEM((every, quarter), bf16)] * 3,
            *[pltpu.VMEM((2, every, quarter), bf16)] * 2,
            *[pltpu.VMEM((rows, quarter), bf16)] * 4,
            dma((12,)),
            dma((4, group)),
            dma((4, group)),
            *[dma((4, 2))] * 2,
            *[dma((4, 4))] * 2,
            dma((4, group)),
            dma((4, group)),
            dma((12,)),
            dma((12,)),
        ],
        compiler_params=pltpu.CompilerParams(collective_id=0, has_side_effects=True, vmem_limit_bytes=61 * 1024 * 1024),
        interpret=interpret,
    )(expert_ids[0].T, gate_levels[0].T, tokens[0], gain, w_gate[0], w_up[0], w_down[0])
    return out[None]


def solution(mesh, interpret=False):
    sizes = (mesh.shape["pipe"], mesh.shape["expert"], mesh.shape["dp"])
    return jax.shard_map(
        functools.partial(body, sizes, interpret),
        mesh=mesh,
        in_specs=(
            P("pipe", "expert", "dp"),
            P("pipe", "expert", None),
            P("pipe", "expert", None),
            P("dp"),
            P("expert", None, "dp"),
            P("expert", None, "dp"),
            P("expert", "dp", None),
        ),
        out_specs=P("pipe", "expert", "dp"),
        check_vma=False,
    )
```
